32 devices in a mesh: groups: 2 (over y), tm: 4 (over z), tok: 4 (over x, core).
Axes of the slice: x: 2, y: 2, z: 4, core: 2. Of those that a mesh axis runs over, the one named last changes fastest.
Arguments:
- queries: bfloat16 [8, 4096, 2048], P(('groups', 'tm'), 'tok'), parts along dimension 0, may hold values from -6 to 6
- keys: bfloat16 [8, 4096, 2048], P(('groups', 'tm'), 'tok'), parts along dimension 0, may hold values from -6 to 6
- values: bfloat16 [8, 4096, 2048], P(('groups', 'tm'), 'tok'), parts along dimension 0, may hold values from -6 to 6
- block_index: int32 [8, 32, 12], P(('groups', 'tm')), parts along dimension 0, may hold values from 0 to 31, all different within a row
- norm_gain: bfloat16 [2048], P('tok'), may hold values from 0.25 to 1.75
- out_weight: bfloat16 [2048, 2048], P('tok'), may hold values from -0.125 to 0.125
Outputs:
- projected: bfloat16 [8, 4096, 2048], P(('groups', 'tm'), 'tok'), parts along dimension 0
The draws below stay inside these ranges and needn't reach their ends.
There are 2 independent parts, one for each index of `groups`. The reference program is written for one: setup_inputs(seed, part) draws one part's arguments, and reference() takes and returns one part's arrays. A program takes and returns all parts, laid end to end along the dimension named above; an argument that names none is the same for every part. Nothing has to cross between parts.
Inputs may be any that keep to these rules, and one draw needn't show every extreme that they name: block_index[t, b, :] holds 12 different block numbers of frame t; every block number appears somewhere.
All inputs are finite; a program needn't handle non-finite values.
Results may differ from the reference program's by a relative error of at most 0.0058.
Values may be sent and summed in bfloat16 or wider, within the bound.
A program may use at most 128 MiB of HBM per device.

```python
import jax
import jax.numpy as jnp
from jax import lax

HEADS = 16
HEAD_DIM = 128
D = 2048
BLK = 128
NB = 32
TOK_FRAME = 4096
KBLK = 12
F_DEV = 1
FRAMES = 4
N_TM = 4


def level_of(key, dims, pieces, least, top_value):
    factor_of, own = 1.0, jax.random.fold_in(key, 6)
    for position, shards_of in pieces:
        heights = jnp.exp(jax.random.uniform(jax.random.fold_in(own, position), (shards_of,), jnp.float32, least / len(pieces), top_value / len(pieces)))
        factor_of = factor_of * jnp.repeat(heights, dims[position] // shards_of).reshape([-1 if axis == position else 1 for axis in range(len(dims))])
    return factor_of


def choose_distinct(stream_key, rows, amount, top, lift):
    order = jax.random.permutation(jax.random.fold_in(stream_key, 1), amount)
    boost = order
    for power in range(3):
        boost = boost * boost // amount
    boost = boost * lift // amount
    lots = jax.random.randint(jax.random.fold_in(stream_key, 2), (rows, amount), 0, 4096) + boost
    sure = jax.random.permutation(jax.random.fold_in(stream_key, 3), rows)[jnp.arange(amount) % rows]
    lots = jnp.where(jnp.arange(rows)[:, None] == sure[None, :], 1 << 14, lots)
    score = lots * amount + jnp.arange(amount)
    return lax.top_k(score.astype(jnp.int32), top)[1].astype(jnp.int32)


def gaussian(rng, dims, deviation, reach, cuts=(), kind=jnp.bfloat16):
    level = level_of(rng, dims, cuts, -0.22, 0.18) if cuts else 1.0
    array = jax.random.normal(rng, dims, jnp.float32) * deviation * level
    return jnp.minimum(jnp.maximum(array, -reach), reach).astype(kind)


def setup_inputs(seed: int = 0, part: int = 0) -> dict:
    splits = jax.random.split(jax.random.key(seed), 7)
    part_splits = jax.random.split(jax.random.fold_in(splits[6], part), 7)
    queries = gaussian(part_splits[0], (FRAMES, TOK_FRAME, D), 1.0, 6.0, ((0, 4), (1, 4)))
    keys = gaussian(part_splits[1], (FRAMES, TOK_FRAME, D), 1.0, 6.0, ((0, 4), (1, 4)))
    values = gaussian(part_splits[2], (FRAMES, TOK_FRAME, D), 1.0, 6.0, ((0, 4), (1, 4)))
    block_index = choose_distinct(part_splits[3], FRAMES * NB, NB, KBLK, 0).reshape((FRAMES, NB, KBLK))
    norm_gain = jnp.clip(1.0 + 0.15 * jax.random.normal(splits[4], (D,), jnp.float32), 0.25, 1.75).astype(jnp.bfloat16)
    out_weight = gaussian(splits[5], (D, D), D ** -0.5, 0.125, ((0, 4),))
    return dict(queries=queries, keys=keys, values=values, block_index=block_index, norm_gain=norm_gain, out_weight=out_weight)


def reference(queries, keys, values, block_index, norm_gain, out_weight):
    query_heads = queries.reshape(FRAMES, TOK_FRAME, HEADS, HEAD_DIM)
    key_heads = keys.reshape(FRAMES, TOK_FRAME, HEADS, HEAD_DIM)
    value_heads = values.reshape(FRAMES, TOK_FRAME, HEADS, HEAD_DIM)

    def frame_product(pair):
        key_frame, value_frame = pair
        return jnp.einsum('thc,thd->hcd', key_frame.astype(jnp.float32), value_frame.astype(jnp.float32))
    frame_state = lax.map(frame_product, (key_heads, value_heads))
    section_sum = lax.optimization_barrier(jnp.sum(frame_state.reshape(N_TM, F_DEV, HEADS, HEAD_DIM, HEAD_DIM), axis=1))
    running = jnp.cumsum(section_sum, axis=0)
    carried = jnp.concatenate([jnp.zeros((1, HEADS, HEAD_DIM, HEAD_DIM), jnp.float32), running[:-1]], axis=0)
    carried = lax.optimization_barrier(carried.astype(jnp.bfloat16)).astype(jnp.float32)
    carried_frame = jnp.repeat(carried, F_DEV, axis=0)
    gain = norm_gain.astype(jnp.float32).reshape(HEADS, HEAD_DIM)
    query_blocks = query_heads.reshape(FRAMES * NB, BLK, HEADS, HEAD_DIM)
    key_blocks = key_heads.reshape(FRAMES, NB, BLK, HEADS, HEAD_DIM)
    value_blocks = value_heads.reshape(FRAMES, NB, BLK, HEADS, HEAD_DIM)
    chosen_all = block_index.reshape(FRAMES * NB, KBLK)
    frame_ids = jnp.arange(FRAMES * NB, dtype=jnp.int32) // NB

    def one_block(item):
        query_part, chosen, frame_id = item
        key_sel = key_blocks[frame_id][chosen].astype(jnp.float32)
        value_sel = value_blocks[frame_id][chosen].astype(jnp.float32)
        query_f = query_part.astype(jnp.float32)
        weight = jnp.einsum('bhc,kjhc->hbkj', query_f, key_sel)
        weight = lax.optimization_barrier(weight.astype(jnp.bfloat16)).astype(jnp.float32)
        intra = jnp.einsum('hbkj,kjhd->bhd', weight, value_sel)
        inter = jnp.einsum('bhc,hcd->bhd', query_f, carried_frame[frame_id])
        mixed = intra + inter
        scale = lax.rsqrt(lax.optimization_barrier(jnp.mean(mixed * mixed, axis=-1, keepdims=True)) + 1e-06)
        return (mixed * scale * gain).astype(jnp.bfloat16)
    attended = lax.map(one_block, (query_blocks, chosen_all, frame_ids))
    attended = attended.reshape(FRAMES * TOK_FRAME, D)
    projected = jnp.dot(attended, out_weight, preferred_element_type=jnp.float32).astype(jnp.bfloat16)
    return projected.reshape(FRAMES, TOK_FRAME, D)
```

```python
import functools

import jax
import jax.numpy as jnp
from jax import lax
from jax.experimental import pallas as pl
from jax.experimental.pallas import tpu as pltpu
from jax.sharding import PartitionSpec as P

HEAD_DIM = 128
BLK = 128
GROUP_HEADS = 2
MESH = pl.DeviceIdType.MESH


def mix_kernel(
    n_tok, n_tm, groups, kblk,
    index_ref, gain_in, q_hbm, k_hbm, v_hbm, out_hbm, *scratch,
):
    states = scratch[:groups]
    (
        kbuf, vbuf, qbuf, att, gain, state_out, state_in, carried,
        in_sem, gain_local, gain_send, gain_recv, far_send, far_recv, near_send, near_recv,
        fwd_send, fwd_recv, st_send, st_recv, out_sem,
    ) = scratch[groups:]
    rows = kbuf.shape[0]
    per_dev = rows // BLK
    heads_dev = gain.shape[2] // HEAD_DIM
    width = GROUP_HEADS * HEAD_DIM
    chips = n_tok // 2
    tok = lax.axis_index("tok")
    tm = lax.axis_index("tm")
    chip, core = tok // 2, tok % 2
    sibling = chip * 2 + (1 - core)

    def far(step):
        return lax.rem(chip + step, chips) * 2 + core

    def far_source(step):
        return lax.rem(chip + chips - step, chips) * 2 + core

    barrier = pltpu.get_barrier_semaphore()
    for step in range(1, n_tok):
        pl.semaphore_signal(
            barrier, inc=1, device_id={"tok": lax.rem(tok + step, n_tok)}, device_id_type=MESH
        )
    for step in range(1, n_tm):
        pl.semaphore_signal(
            barrier, inc=1, device_id={"tm": lax.rem(tm + step, n_tm)}, device_id_type=MESH
        )

    def load(g, which):
        source, target = ((k_hbm, kbuf), (v_hbm, vbuf), (q_hbm, qbuf))[which]
        cols = pl.ds(g * width, width)
        return pltpu.make_async_copy(
            source.at[0, :, cols], target.at[:, cols], in_sem.at[which, g]
        )

    for g in range(groups):
        load(g, 0).start()
        load(g, 1).start()
    for g in range(groups):
        load(g, 2).start()
    own_gain = pltpu.make_async_copy(gain_in, gain.at[tok], gain_local)
    own_gain.start()
    pl.semaphore_wait(barrier, n_tok - 1 + n_tm - 1)

    def gain_copy(step, source):
        return pltpu.make_async_remote_copy(
            src_ref=gain_in, dst_ref=gain.at[source], send_sem=gain_send.at[step],
            recv_sem=gain_recv.at[step], device_id={"tok": lax.rem(tok + step, n_tok)},
            device_id_type=MESH,
        )

    for step in range(1, n_tok):
        gain_copy(step, tok).start()

    def piece(g, owner):
        return states[g].at[pl.ds(owner * per_dev, per_dev)]

    def far_copy(g, step, owner):
        return pltpu.make_async_remote_copy(
            src_ref=piece(g, owner), dst_ref=piece(g, owner), send_sem=far_send.at[g, step],
            recv_sem=far_recv.at[g, step], device_id={"tok": far(step)}, device_id_type=MESH,
        )

    def near_copy(g, owner):
        return pltpu.make_async_remote_copy(
            src_ref=piece(g, owner), dst_ref=piece(g, owner), send_sem=near_send.at[g],
            recv_sem=near_recv.at[g], device_id={"tok": sibling}, device_id_type=MESH,
        )

    def forward_copy(g, step, owner):
        return pltpu.make_async_remote_copy(
            src_ref=piece(g, owner), dst_ref=piece(g, owner), send_sem=fwd_send.at[g, step],
            recv_sem=fwd_recv.at[g, step], device_id={"tok": sibling}, device_id_type=MESH,
        )

    def state_copy(g, step):
        return pltpu.make_async_remote_copy(
            src_ref=state_out.at[g], dst_ref=state_in.at[g, step], send_sem=st_send.at[g, step],
            recv_sem=st_recv.at[g, step], device_id={"tm": lax.rem(tm + step, n_tm)},
            device_id_type=MESH,
        )

    for g in range(groups):
        load(g, 0).wait()
        load(g, 1).wait()

        def block_state(j, _, g=g):
            at = pl.ds(pl.multiple_of(j * BLK, BLK), BLK)
            for h in range(GROUP_HEADS):
                cols = pl.ds(g * width + h * HEAD_DIM, HEAD_DIM)
                product = lax.dot_general(
                    kbuf[at, cols], vbuf[at, cols], (((0,), (0,)), ((), ())),
                    preferred_element_type=jnp.float32,
                )
                states[g][tok * per_dev + j, h] = product.astype(jnp.bfloat16)
            return 0

        lax.fori_loop(0, per_dev, block_state, 0)
        for step in range(1, chips):
            far_copy(g, step, tok).start()
        near_copy(g, tok).start()

    own_gain.wait()
    for step in range(1, n_tok):
        gain_copy(step, lax.rem(tok + n_tok - step, n_tok)).wait_recv()

    def arrive(g):
        for step in range(1, chips):
            far_copy(g, step, far_source(step)).wait_recv()
            forward_copy(g, step, far_source(step)).start()

    def frame_state(g):
        near_copy(g, sibling).wait_recv()
        for step in range(1, chips):
            source = lax.rem(chip + chips - step, chips) * 2 + (1 - core)
            forward_copy(g, step, source).wait_recv()
        for h in range(GROUP_HEADS):
            def add(n, total, h=h):
                for u in range(4):
                    total = total + states[g][n * 4 + u, h].astype(jnp.float32)
                return total

            total = lax.fori_loop(
                0, n_tok * per_dev // 4, add, jnp.zeros((HEAD_DIM, HEAD_DIM), jnp.float32)
            )
            state_out[g, h] = total.astype(jnp.bfloat16)
        for step in range(1, n_tm):
            state_copy(g, step).start()

    def attend(g):
        load(g, 2).wait()
        for step in range(1, n_tm):
            state_copy(g, step).wait_recv()
        for h in range(GROUP_HEADS):
            total = jnp.zeros((HEAD_DIM, HEAD_DIM), jnp.float32)
            for step in range(1, n_tm):
                earlier = (tm >= step).astype(jnp.float32)
                total = total + state_in[g, step, h].astype(jnp.float32) * earlier
            carried[h] = total

        def block(b, _):
            at = pl.ds(pl.multiple_of(b * BLK, BLK), BLK)
            chosen = [index_ref[0, tok * per_dev + b, i] for i in range(kblk)]
            for h in range(GROUP_HEADS):
                head = g * GROUP_HEADS + h
                cols = pl.ds(head * HEAD_DIM, HEAD_DIM)
                total = carried[h]
                for i in range(kblk):
                    total = total + states[g][chosen[i], h].astype(jnp.float32)
                mixed = jnp.dot(
                    qbuf[at, cols], total.astype(jnp.bfloat16), preferred_element_type=jnp.float32
                )
                scale = lax.rsqrt(jnp.mean(mixed * mixed, axis=-1, keepdims=True) + 1e-06)
                g_row = gain[head // heads_dev, 0:1, pl.ds((head % heads_dev) * HEAD_DIM, HEAD_DIM)]
                att[at, cols] = (mixed * scale * g_row).astype(jnp.bfloat16)
            return 0

        lax.fori_loop(0, per_dev, block, 0)
        store(g).start()

    def store(g):
        cols = pl.ds(g * width, width)
        return pltpu.make_async_copy(att.at[:, cols], out_hbm.at[:, cols], out_sem.at[g])

    for turn in range(groups + 2):
        if turn < groups:
            arrive(turn)
        if 0 <= turn - 1 < groups:
            frame_state(turn - 1)
        if 0 <= turn - 2 < groups:
            attend(turn - 2)

    for g in range(groups):
        store(g).wait()
        near_copy(g, tok).wait_send()
        for step in range(1, chips):
            far_copy(g, step, tok).wait_send()
            forward_copy(g, step, far_source(step)).wait_send()
        for step in range(1, n_tm):
            state_copy(g, step).wait_send()
    for step in range(1, n_tok):
        gain_copy(step, tok).wait_send()


def on_device(n_tok, n_tm, queries, keys, values, block_index, norm_gain, out_weight):
    rows, model_width = queries.shape[1:]
    kblk = block_index.shape[2]
    heads = model_width // HEAD_DIM
    groups = heads // GROUP_HEADS
    chips = n_tok // 2
    blocks = n_tok * rows // BLK
    gain_rows = jnp.broadcast_to(norm_gain.astype(jnp.float32)[None], (8, norm_gain.shape[0]))
    weight = lax.all_gather(out_weight, "tok", axis=0, tiled=True)
    dma = pltpu.SemaphoreType.DMA
    attended = pl.pallas_call(
        functools.partial(mix_kernel, n_tok, n_tm, groups, kblk),
        out_shape=jax.ShapeDtypeStruct((rows, model_width), jnp.bfloat16),
        in_specs=[
            pl.BlockSpec(memory_space=pltpu.SMEM),
            pl.BlockSpec(memory_space=pltpu.VMEM),
            pl.BlockSpec(memory_space=pl.ANY),
            pl.BlockSpec(memory_space=pl.ANY),
            pl.BlockSpec(memory_space=pl.ANY),
        ],
        out_specs=pl.BlockSpec(memory_space=pl.ANY),
        scratch_shapes=[
            pltpu.VMEM((blocks, GROUP_HEADS, HEAD_DIM, HEAD_DIM), jnp.bfloat16)
            for _ in range(groups)
        ] + [
            pltpu.VMEM((rows, model_width), jnp.bfloat16),
            pltpu.VMEM((rows, model_width), jnp.bfloat16),
            pltpu.VMEM((rows, model_width), jnp.bfloat16),
            pltpu.VMEM((rows, model_width), jnp.bfloat16),
            pltpu.VMEM((n_tok,) + gain_rows.shape, jnp.float32),
            pltpu.VMEM((groups, GROUP_HEADS, HEAD_DIM, HEAD_DIM), jnp.bfloat16),
            pltpu.VMEM((groups, n_tm, GROUP_HEADS, HEAD_DIM, HEAD_DIM), jnp.bfloat16),
            pltpu.VMEM((GROUP_HEADS, HEAD_DIM, HEAD_DIM), jnp.float32),
            dma((3, groups)),
            dma(()),
            dma((n_tok,)),
            dma((n_tok,)),
            dma((groups, chips)),
            dma((groups, chips)),
            dma((groups,)),
            dma((groups,)),
            dma((groups, chips)),
            dma((groups, chips)),
            dma((groups, n_tm)),
            dma((groups, n_tm)),
            dma((groups,)),
        ],
        compiler_params=pltpu.CompilerParams(
            collective_id=0, has_side_effects=True, vmem_limit_bytes=56 * 1024 * 1024
        ),
        cost_estimate=pl.CostEstimate(
            flops=8 * rows * model_width * HEAD_DIM, bytes_accessed=400_000_000, transcendentals=0
        ),
    )(block_index, gain_rows, queries, keys, values)
    total = jnp.dot(attended, weight, preferred_element_type=jnp.float32)
    return total.astype(jnp.bfloat16)[None]


def solution(mesh):
    in_specs = (
        P(("groups", "tm"), "tok", None),
        P(("groups", "tm"), "tok", None),
        P(("groups", "tm"), "tok", None),
        P(("groups", "tm"), None, None),
        P("tok"),
        P("tok", None),
    )
    out_specs = P(("groups", "tm"), "tok", None)
    return jax.shard_map(
        functools.partial(on_device, mesh.shape["tok"], mesh.shape["tm"]),
        mesh=mesh, in_specs=in_specs, out_specs=out_specs, check_vma=False,
    )
```

```python
import functools

import jax
import jax.numpy as jnp
from jax import lax
from jax.experimental import pallas as pl
from jax.experimental.pallas import tpu as pltpu
from jax.sharding import PartitionSpec as P

HEAD_DIM = 128
BLK = 128
GROUP_HEADS = 2
MESH = pl.DeviceIdType.MESH


def mix_kernel(
    n_tok, n_tm, columns, groups, kblk,
    index_ref, gain_in, q_hbm, k_hbm, v_hbm, w_hbm, out_hbm, *scratch,
):
    states = scratch[:groups]
    (
        kbuf, vbuf, qbuf, att, weight, acc, gain, state_out, state_in, carried,
        in_sem, gain_local, gain_send, gain_recv, far_send, far_recv, near_send, near_recv,
        fwd_send, fwd_recv, st_send, st_recv, out_sem,
        w_local, ws_send, ws_recv, wf_send, wf_recv, wb_send, wb_recv, wn_send, wn_recv,
    ) = scratch[groups:]
    rows = kbuf.shape[0]
    per_dev = rows // BLK
    heads_dev = gain.shape[2] // HEAD_DIM
    width = GROUP_HEADS * HEAD_DIM
    chips = n_tok // 2
    tok = lax.axis_index("tok")
    tm = lax.axis_index("tm")
    chip, core = tok // 2, tok % 2
    sibling = chip * 2 + (1 - core)
    column = lax.axis_index("groups") * n_tm + tm
    w_rows = w_hbm.shape[0]
    w_cols = weight.shape[2]
    tile = min(rows, 256)

    def column_peer(step):
        peer = lax.rem(column + step, columns)
        return {"groups": peer // n_tm, "tm": peer % n_tm}

    def column_source(step):
        return lax.rem(column + columns - step, columns)

    def far(step):
        return lax.rem(chip + step, chips) * 2 + core

    def far_source(step):
        return lax.rem(chip + chips - step, chips) * 2 + core

    barrier = pltpu.get_barrier_semaphore()
    for step in range(1, n_tok):
        pl.semaphore_signal(
            barrier, inc=1, device_id={"tok": lax.rem(tok + step, n_tok)}, device_id_type=MESH
        )
    for step in range(1, columns):
        pl.semaphore_signal(barrier, inc=1, device_id=column_peer(step), device_id_type=MESH)

    def load(g, which):
        source, target = ((k_hbm, kbuf), (v_hbm, vbuf), (q_hbm, qbuf))[which]
        cols = pl.ds(g * width, width)
        return pltpu.make_async_copy(
            source.at[0, :, cols], target.at[:, cols], in_sem.at[which, g]
        )

    for g in range(groups):
        load(g, 0).start()
        load(g, 1).start()
    for g in range(groups):
        load(g, 2).start()
    own_gain = pltpu.make_async_copy(gain_in, gain.at[tok], gain_local)
    own_gain.start()
    pl.semaphore_wait(barrier, n_tok - 1 + columns - 1)

    def w_part(part, owner):
        return weight.at[part, pl.ds(pl.multiple_of(owner * w_rows, w_rows), w_rows)]

    def w_source(part):
        return w_hbm.at[:, pl.ds(pl.multiple_of(part * w_cols, w_cols), w_cols)]

    def w_local_copy(part):
        return pltpu.make_async_copy(w_source(part), w_part(part, tok), w_local.at[part])

    def w_near_copy(part, owner):
        return pltpu.make_async_remote_copy(
            src_ref=w_source(part), dst_ref=w_part(part, owner), send_sem=ws_send.at[part],
            recv_sem=ws_recv.at[part], device_id={"tok": sibling}, device_id_type=MESH,
        )

    def w_far_copy(step, owner):
        return pltpu.make_async_remote_copy(
            src_ref=w_source(column), dst_ref=w_part(column, owner), send_sem=wf_send.at[step],
            recv_sem=wf_recv.at[step], device_id={"tok": far(step)}, device_id_type=MESH,
        )

    def w_spread_copy(step, hop, part):
        return pltpu.make_async_remote_copy(
            src_ref=w_part(part, far_source(step)), dst_ref=w_part(part, far_source(step)),
            send_sem=wb_send.at[step, hop], recv_sem=wb_recv.at[step, hop],
            device_id=column_peer(hop), device_id_type=MESH,
        )

    def w_forward_copy(step, hop, owner):
        part = column_source(hop)
        return pltpu.make_async_remote_copy(
            src_ref=w_part(part, owner), dst_ref=w_part(part, owner),
            send_sem=wn_send.at[step, hop], recv_sem=wn_recv.at[step, hop],
            device_id={"tok": sibling}, device_id_type=MESH,
        )

    for step in range(1, chips):
        w_far_copy(step, tok).start()

    def gain_copy(step, source):
        return pltpu.make_async_remote_copy(
            src_ref=gain_in, dst_ref=gain.at[source], send_sem=gain_send.at[step],
            recv_sem=gain_recv.at[step], device_id={"tok": lax.rem(tok + step, n_tok)},
            device_id_type=MESH,
        )

    for step in range(1, n_tok):
        gain_copy(step, tok).start()

    def piece(g, owner):
        return states[g].at[pl.ds(owner * per_dev, per_dev)]

    def far_copy(g, step, owner):
        return pltpu.make_async_remote_copy(
            src_ref=piece(g, owner), dst_ref=piece(g, owner), send_sem=far_send.at[g, step],
            recv_sem=far_recv.at[g, step], device_id={"tok": far(step)}, device_id_type=MESH,
        )

    def near_copy(g, owner):
        return pltpu.make_async_remote_copy(
            src_ref=piece(g, owner), dst_ref=piece(g, owner), send_sem=near_send.at[g],
            recv_sem=near_recv.at[g], device_id={"tok": sibling}, device_id_type=MESH,
        )

    def forward_copy(g, step, owner):
        return pltpu.make_async_remote_copy(
            src_ref=piece(g, owner), dst_ref=piece(g, owner), send_sem=fwd_send.at[g, step],
            recv_sem=fwd_recv.at[g, step], device_id={"tok": sibling}, device_id_type=MESH,
        )

    def state_copy(g, step):
        return pltpu.make_async_remote_copy(
            src_ref=state_out.at[g], dst_ref=state_in.at[g, step], send_sem=st_send.at[g, step],
            recv_sem=st_recv.at[g, step], device_id={"tm": lax.rem(tm + step, n_tm)},
            device_id_type=MESH,
        )

    for g in range(groups):
        load(g, 0).wait()
        load(g, 1).wait()

        def block_state(j, _, g=g):
            at = pl.ds(pl.multiple_of(j * BLK, BLK), BLK)
            for h in range(GROUP_HEADS):
                cols = pl.ds(g * width + h * HEAD_DIM, HEAD_DIM)
                product = lax.dot_general(
                    kbuf[at, cols], vbuf[at, cols], (((0,), (0,)), ((), ())),
                    preferred_element_type=jnp.float32,
                )
                states[g][tok * per_dev + j, h] = product.astype(jnp.bfloat16)
            return 0

        lax.fori_loop(0, per_dev, block_state, 0)
        for step in range(1, chips):
            far_copy(g, step, tok).start()
        near_copy(g, tok).start()

    for step in range(1, chips):
        w_far_copy(step, far_source(step)).wait_recv()
        for hop in range(1, columns):
            w_spread_copy(step, hop, column).start()
    for part in range(columns):
        w_local_copy(part).start()
        w_near_copy(part, tok).start()

    own_gain.wait()
    for step in range(1, n_tok):
        gain_copy(step, lax.rem(tok + n_tok - step, n_tok)).wait_recv()

    def arrive(g):
        for step in range(1, chips):
            far_copy(g, step, far_source(step)).wait_recv()
            forward_copy(g, step, far_source(step)).start()

    def frame_state(g):
        near_copy(g, sibling).wait_recv()
        for step in range(1, chips):
            source = lax.rem(chip + chips - step, chips) * 2 + (1 - core)
            forward_copy(g, step, source).wait_recv()
        for h in range(GROUP_HEADS):
            def add(n, total, h=h):
                for u in range(4):
                    total = total + states[g][n * 4 + u, h].astype(jnp.float32)
                return total

            total = lax.fori_loop(
                0, n_tok * per_dev // 4, add, jnp.zeros((HEAD_DIM, HEAD_DIM), jnp.float32)
            )
            state_out[g, h] = total.astype(jnp.bfloat16)
        for step in range(1, n_tm):
            state_copy(g, step).start()

    def attend(g):
        load(g, 2).wait()
        for step in range(1, n_tm):
            state_copy(g, step).wait_recv()
        for h in range(GROUP_HEADS):
            total = jnp.zeros((HEAD_DIM, HEAD_DIM), jnp.float32)
            for step in range(1, n_tm):
                earlier = (tm >= step).astype(jnp.float32)
                total = total + state_in[g, step, h].astype(jnp.float32) * earlier
            carried[h] = total

        def block(b, _):
            at = pl.ds(pl.multiple_of(b * BLK, BLK), BLK)
            chosen = [index_ref[0, tok * per_dev + b, i] for i in range(kblk)]
            for h in range(GROUP_HEADS):
                head = g * GROUP_HEADS + h
                cols = pl.ds(head * HEAD_DIM, HEAD_DIM)
                total = carried[h]
                for i in range(kblk):
                    total = total + states[g][chosen[i], h].astype(jnp.float32)
                high = total.astype(jnp.bfloat16)
                low = (total - high.astype(jnp.float32)).astype(jnp.bfloat16)
                q_block = qbuf[at, cols]
                mixed = jnp.dot(
                    jnp.concatenate([q_block, q_block], axis=1),
                    jnp.concatenate([high, low], axis=0),
                    preferred_element_type=jnp.float32,
                )
                scale = lax.rsqrt(jnp.mean(mixed * mixed, axis=-1, keepdims=True) + 1e-06)
                g_row = gain[head // heads_dev, 0:1, pl.ds((head % heads_dev) * HEAD_DIM, HEAD_DIM)]
                att[at, cols] = (mixed * scale * g_row).astype(jnp.bfloat16)
            return 0

        lax.fori_loop(0, per_dev, block, 0)

    def forward_weight():
        for step in range(1, chips):
            for hop in range(columns):
                if hop:
                    w_spread_copy(step, hop, column_source(hop)).wait_recv()
                w_forward_copy(step, hop, far_source(step)).start()

    def await_weight():
        for part in range(columns):
            w_local_copy(part).wait()
            w_near_copy(part, sibling).wait_recv()
        for step in range(1, chips):
            for hop in range(columns):
                source = lax.rem(chip + chips - step, chips) * 2 + (1 - core)
                w_forward_copy(step, hop, source).wait_recv()

    def store(r):
        at = pl.ds(pl.multiple_of(r * tile, tile), tile)
        return pltpu.make_async_copy(kbuf.at[at], out_hbm.at[0, at], out_sem.at[r])

    def project(low, high, first=False, last=False):
        depth = pl.ds(low * width, (high - low) * width)

        def row_tile(r, _):
            at = pl.ds(pl.multiple_of(r * tile, tile), tile)

            def part_of(part, _):
                cols = pl.ds(pl.multiple_of(part * w_cols, w_cols), w_cols)
                total = jnp.dot(
                    att[at, depth], weight[part, depth, :], preferred_element_type=jnp.float32
                )
                if not first:
                    total = total + acc[at, cols]
                if last:
                    kbuf[at, cols] = total.astype(jnp.bfloat16)
                else:
                    acc[at, cols] = total
                return 0

            lax.fori_loop(0, columns, part_of, 0)
            if last:
                store(r).start()
            return 0

        lax.fori_loop(0, rows // tile, row_tile, 0)

    half = groups // 2
    for turn in range(groups + 2):
        if 0 <= turn - 1 < groups:
            frame_state(turn - 1)
        if 0 <= turn - 2 < groups:
            attend(turn - 2)
        if turn == half:
            forward_weight()
        if turn == half + 1:
            await_weight()
            project(0, half, first=True)
        if turn > half + 1:
            project(turn - 2, turn - 1, last=turn == groups + 1)
        if turn < groups:
            arrive(turn)

    for r in range(rows // tile):
        store(r).wait()
    for part in range(columns):
        w_near_copy(part, tok).wait_send()
    for step in range(1, chips):
        w_far_copy(step, tok).wait_send()
        for hop in range(columns):
            if hop:
                w_spread_copy(step, hop, column).wait_send()
            w_forward_copy(step, hop, far_source(step)).wait_send()
    for g in range(groups):
        near_copy(g, tok).wait_send()
        for step in range(1, chips):
            far_copy(g, step, tok).wait_send()
            forward_copy(g, step, far_source(step)).wait_send()
        for step in range(1, n_tm):
            state_copy(g, step).wait_send()
    for step in range(1, n_tok):
        gain_copy(step, tok).wait_send()


def on_device(n_tok, n_tm, columns, queries, keys, values, block_index, norm_gain, out_weight):
    rows, model_width = queries.shape[1:]
    kblk = block_index.shape[2]
    heads = model_width // HEAD_DIM
    groups = heads // GROUP_HEADS
    chips = n_tok // 2
    blocks = n_tok * rows // BLK
    gain_rows = jnp.broadcast_to(norm_gain.astype(jnp.float32)[None], (8, norm_gain.shape[0]))
    dma = pltpu.SemaphoreType.DMA
    return pl.pallas_call(
        functools.partial(mix_kernel, n_tok, n_tm, columns, groups, kblk),
        out_shape=jax.ShapeDtypeStruct((1, rows, model_width), jnp.bfloat16),
        in_specs=[
            pl.BlockSpec(memory_space=pltpu.SMEM),
            pl.BlockSpec(memory_space=pltpu.VMEM),
            pl.BlockSpec(memory_space=pl.ANY),
            pl.BlockSpec(memory_space=pl.ANY),
            pl.BlockSpec(memory_space=pl.ANY),
            pl.BlockSpec(memory_space=pl.ANY),
        ],
        out_specs=pl.BlockSpec(memory_space=pl.ANY),
        scratch_shapes=[
            pltpu.VMEM((blocks, GROUP_HEADS, HEAD_DIM, HEAD_DIM), jnp.bfloat16)
            for _ in range(groups)
        ] + [
            pltpu.VMEM((rows, model_width), jnp.bfloat16),
            pltpu.VMEM((rows, model_width), jnp.bfloat16),
            pltpu.VMEM((rows, model_width), jnp.bfloat16),
            pltpu.VMEM((rows, model_width), jnp.bfloat16),
            pltpu.VMEM((columns, model_width, model_width // columns), jnp.bfloat16),
            pltpu.VMEM((rows, model_width), jnp.float32),
            pltpu.VMEM((n_tok,) + gain_rows.shape, jnp.float32),
            pltpu.VMEM((groups, GROUP_HEADS, HEAD_DIM, HEAD_DIM), jnp.bfloat16),
            pltpu.VMEM((groups, n_tm, GROUP_HEADS, HEAD_DIM, HEAD_DIM), jnp.bfloat16),
            pltpu.VMEM((GROUP_HEADS, HEAD_DIM, HEAD_DIM), jnp.float32),
            dma((3, groups)),
            dma(()),
            dma((n_tok,)),
            dma((n_tok,)),
            dma((groups, chips)),
            dma((groups, chips)),
            dma((groups,)),
            dma((groups,)),
            dma((groups, chips)),
            dma((groups, chips)),
            dma((groups, n_tm)),
            dma((groups, n_tm)),
            dma((rows // min(rows, 256),)),
            dma((columns,)),
            dma((columns,)),
            dma((columns,)),
            dma((chips,)),
            dma((chips,)),
            dma((chips, columns)),
            dma((chips, columns)),
            dma((chips, columns)),
            dma((chips, columns)),
        ],
        compiler_params=pltpu.CompilerParams(
            collective_id=0, has_side_effects=True, vmem_limit_bytes=60 * 1024 * 1024
        ),
        cost_estimate=pl.CostEstimate(
            flops=8 * rows * model_width * HEAD_DIM, bytes_accessed=400_000_000, transcendentals=0
        ),
    )(block_index, gain_rows, queries, keys, values, out_weight)


def solution(mesh):
    in_specs = (
        P(("groups", "tm"), "tok", None),
        P(("groups", "tm"), "tok", None),
        P(("groups", "tm"), "tok", None),
        P(("groups", "tm"), None, None),
        P("tok"),
        P("tok", None),
    )
    out_specs = P(("groups", "tm"), "tok", None)
    return jax.shard_map(
        functools.partial(on_device, mesh.shape["tok"], mesh.shape["tm"], mesh.shape["groups"] * mesh.shape["tm"]),
        mesh=mesh, in_specs=in_specs, out_specs=out_specs, check_vma=False,
    )
```

```python
import functools

import jax
import jax.numpy as jnp
from jax import lax
from jax.experimental import pallas as pl
from jax.experimental.pallas import tpu as pltpu
from jax.sharding import PartitionSpec as P

HEAD_DIM = 128
BLK = 128
GROUP_HEADS = 2
MESH = pl.DeviceIdType.MESH


def mix_kernel(
    n_tok, n_tm, columns, groups, kblk,
    index_ref, gain_in, q_hbm, k_hbm, v_hbm, w_hbm, out_hbm, *scratch,
):
    states = scratch[:groups]
    (
        kbuf, vbuf, qbuf, att, weight, acc, gain, state_out, state_in, carried,
        in_sem, gain_local, gain_send, gain_recv, far_send, far_recv, near_send, near_recv,
        fwd_send, fwd_recv, st_send, st_recv, out_sem,
        w_local, ws_send, ws_recv, wf_send, wf_recv, wb_send, wb_recv, wn_send, wn_recv,
    ) = scratch[groups:]
    rows = kbuf.shape[0]
    per_dev = rows // BLK
    heads_dev = gain.shape[2] // HEAD_DIM
    width = GROUP_HEADS * HEAD_DIM
    chips = n_tok // 2
    tok = lax.axis_index("tok")
    tm = lax.axis_index("tm")
    chip, core = tok // 2, tok % 2
    sibling = chip * 2 + (1 - core)
    w_rows = w_hbm.shape[0]
    w_cols = weight.shape[2]
    scenes = columns // n_tm
    scene = lax.axis_index("groups")
    column = scene * n_tm + tm

    def column_peer(step):
        peer = lax.rem(column + step, columns)
        return {"groups": peer // n_tm, "tm": peer % n_tm}

    def column_source(hop):
        section = lax.rem(tm + n_tm - hop % n_tm, n_tm)
        return lax.rem(scene + scenes - hop // n_tm, scenes) * n_tm + section

    def far(step):
        return lax.rem(chip + step, chips) * 2 + core

    def far_source(step):
        return lax.rem(chip + chips - step, chips) * 2 + core

    barrier = pltpu.get_barrier_semaphore()
    for step in range(1, n_tok):
        pl.semaphore_signal(
            barrier, inc=1, device_id={"tok": lax.rem(tok + step, n_tok)}, device_id_type=MESH
        )
    for step in range(1, columns):
        pl.semaphore_signal(barrier, inc=1, device_id=column_peer(step), device_id_type=MESH)

    def load(g, which):
        source, target = ((k_hbm, kbuf), (v_hbm, vbuf), (q_hbm, qbuf))[which]
        cols = pl.ds(g * width, width)
        return pltpu.make_async_copy(
            source.at[0, :, cols], target.at[:, cols], in_sem.at[which, g]
        )

    for g in range(groups):
        load(g, 0).start()
        load(g, 1).start()
    for g in range(groups):
        load(g, 2).start()
    own_gain = pltpu.make_async_copy(gain_in, gain.at[tok], gain_local)
    own_gain.start()
    pl.semaphore_wait(barrier, n_tok - 1 + columns - 1)

    def w_part(part, owner):
        return weight.at[part, pl.ds(pl.multiple_of(owner * w_rows, w_rows), w_rows)]

    def w_source(part):
        return w_hbm.at[:, pl.ds(pl.multiple_of(part * w_cols, w_cols), w_cols)]

    def w_local_copy(part):
        return pltpu.make_async_copy(w_source(part), w_part(part, tok), w_local.at[part])

    def w_near_copy(part, owner):
        return pltpu.make_async_remote_copy(
            src_ref=w_source(part), dst_ref=w_part(part, owner), send_sem=ws_send.at[part],
            recv_sem=ws_recv.at[part], device_id={"tok": sibling}, device_id_type=MESH,
        )

    def w_far_copy(step, owner):
        return pltpu.make_async_remote_copy(
            src_ref=w_source(column), dst_ref=w_part(column, owner), send_sem=wf_send.at[step],
            recv_sem=wf_recv.at[step], device_id={"tok": far(step)}, device_id_type=MESH,
        )

    def w_spread_copy(step, hop, part):
        if hop < n_tm:
            target = {"tm": lax.rem(tm + hop, n_tm)}
        else:
            target = {"groups": lax.rem(scene + hop // n_tm, scenes)}
        return pltpu.make_async_remote_copy(
            src_ref=w_part(part, far_source(step)), dst_ref=w_part(part, far_source(step)),
            send_sem=wb_send.at[step, hop], recv_sem=wb_recv.at[step, hop],
            device_id=target, device_id_type=MESH,
        )

    def spread_send(step, hop):
        return w_spread_copy(step, hop, column_source(hop % n_tm))

    def spread_tm():
        for step in range(1, chips):
            w_far_copy(step, far_source(step)).wait_recv()
            for hop in range(1, n_tm):
                w_spread_copy(step, hop, column).start()
            for other in range(1, scenes):
                spread_send(step, other * n_tm).start()

    def spread_groups():
        for step in range(1, chips):
            for hop in range(1, n_tm):
                w_spread_copy(step, hop, column_source(hop)).wait_recv()
                for other in range(1, scenes):
                    spread_send(step, other * n_tm + hop).start()

    def w_forward_copy(step, hop, owner):
        part = column_source(hop)
        return pltpu.make_async_remote_copy(
            src_ref=w_part(part, owner), dst_ref=w_part(part, owner),
            send_sem=wn_send.at[step, hop], recv_sem=wn_recv.at[step, hop],
            device_id={"tok": sibling}, device_id_type=MESH,
        )

    for step in range(1, chips):
        w_far_copy(step, tok).start()

    def gain_copy(step, source):
        return pltpu.make_async_remote_copy(
            src_ref=gain_in, dst_ref=gain.at[source], send_sem=gain_send.at[step],
            recv_sem=gain_recv.at[step], device_id={"tok": lax.rem(tok + step, n_tok)},
            device_id_type=MESH,
        )

    for step in range(1, n_tok):
        gain_copy(step, tok).start()

    def piece(g, owner):
        return states[g].at[pl.ds(owner * per_dev, per_dev)]

    def far_copy(g, step, owner):
        return pltpu.make_async_remote_copy(
            src_ref=piece(g, owner), dst_ref=piece(g, owner), send_sem=far_send.at[g, step],
            recv_sem=far_recv.at[g, step], device_id={"tok": far(step)}, device_id_type=MESH,
        )

    def near_copy(g, owner):
        return pltpu.make_async_remote_copy(
            src_ref=piece(g, owner), dst_ref=piece(g, owner), send_sem=near_send.at[g],
            recv_sem=near_recv.at[g], device_id={"tok": sibling}, device_id_type=MESH,
        )

    def forward_copy(g, step, owner):
        return pltpu.make_async_remote_copy(
            src_ref=piece(g, owner), dst_ref=piece(g, owner), send_sem=fwd_send.at[g, step],
            recv_sem=fwd_recv.at[g, step], device_id={"tok": sibling}, device_id_type=MESH,
        )

    def state_copy(g, step):
        return pltpu.make_async_remote_copy(
            src_ref=state_out.at[g], dst_ref=state_in.at[g, step], send_sem=st_send.at[g, step],
            recv_sem=st_recv.at[g, step], device_id={"tm": lax.rem(tm + step, n_tm)},
            device_id_type=MESH,
        )

    for g in range(groups):
        load(g, 0).wait()
        load(g, 1).wait()

        def block_state(j, _, g=g):
            at = pl.ds(pl.multiple_of(j * BLK, BLK), BLK)
            for h in range(GROUP_HEADS):
                cols = pl.ds(g * width + h * HEAD_DIM, HEAD_DIM)
                product = lax.dot_general(
                    kbuf[at, cols], vbuf[at, cols], (((0,), (0,)), ((), ())),
                    preferred_element_type=jnp.float32,
                )
                states[g][tok * per_dev + j, h] = product.astype(jnp.bfloat16)
            return 0

        lax.fori_loop(0, per_dev, block_state, 0)
        for step in range(1, chips):
            far_copy(g, step, tok).start()
        near_copy(g, tok).start()
        if g == 1:
            spread_tm()

    for part in range(columns):
        w_local_copy(part).start()
        w_near_copy(part, tok).start()

    own_gain.wait()
    for step in range(1, n_tok):
        gain_copy(step, lax.rem(tok + n_tok - step, n_tok)).wait_recv()

    def arrive(g):
        for step in range(1, chips):
            far_copy(g, step, far_source(step)).wait_recv()
            forward_copy(g, step, far_source(step)).start()

    def frame_state(g):
        near_copy(g, sibling).wait_recv()
        for step in range(1, chips):
            source = lax.rem(chip + chips - step, chips) * 2 + (1 - core)
            forward_copy(g, step, source).wait_recv()
        for h in range(GROUP_HEADS):
            def add(n, total, h=h):
                for u in range(4):
                    total = total + states[g][n * 4 + u, h].astype(jnp.float32)
                return total

            total = lax.fori_loop(
                0, n_tok * per_dev // 4, add, jnp.zeros((HEAD_DIM, HEAD_DIM), jnp.float32)
            )
            state_out[g, h] = total.astype(jnp.bfloat16)
        for step in range(1, n_tm):
            state_copy(g, step).start()

    def attend(g):
        load(g, 2).wait()
        for step in range(1, n_tm):
            state_copy(g, step).wait_recv()
        for h in range(GROUP_HEADS):
            total = jnp.zeros((HEAD_DIM, HEAD_DIM), jnp.float32)
            for step in range(1, n_tm):
                earlier = (tm >= step).astype(jnp.float32)
                total = total + state_in[g, step, h].astype(jnp.float32) * earlier
            carried[h] = total

        def block(b, _):
            at = pl.ds(pl.multiple_of(b * BLK, BLK), BLK)
            chosen = [index_ref[0, tok * per_dev + b, i] for i in range(kblk)]
            for h in range(GROUP_HEADS):
                head = g * GROUP_HEADS + h
                cols = pl.ds(head * HEAD_DIM, HEAD_DIM)
                total = carried[h]
                for i in range(kblk):
                    total = total + states[g][chosen[i], h].astype(jnp.float32)
                high = total.astype(jnp.bfloat16)
                low = (total - high.astype(jnp.float32)).astype(jnp.bfloat16)
                q_block = qbuf[at, cols]
                mixed = jnp.dot(
                    jnp.concatenate([q_block, q_block], axis=1),
                    jnp.concatenate([high, low], axis=0),
                    preferred_element_type=jnp.float32,
                )
                scale = lax.rsqrt(jnp.mean(mixed * mixed, axis=-1, keepdims=True) + 1e-06)
                g_row = gain[head // heads_dev, 0:1, pl.ds((head % heads_dev) * HEAD_DIM, HEAD_DIM)]
                att[at, cols] = (mixed * scale * g_row).astype(jnp.bfloat16)
            return 0

        lax.fori_loop(0, per_dev, block, 0)

    def forward_weight():
        for step in range(1, chips):
            for hop in range(columns):
                if hop >= n_tm:
                    w_spread_copy(step, hop, column_source(hop)).wait_recv()
                w_forward_copy(step, hop, far_source(step)).start()

    def await_weight():
        for part in range(columns):
            w_local_copy(part).wait()
            w_near_copy(part, sibling).wait_recv()
        for step in range(1, chips):
            for hop in range(columns):
                source = lax.rem(chip + chips - step, chips) * 2 + (1 - core)
                w_forward_copy(step, hop, source).wait_recv()

    def store(part):
        cols = pl.ds(pl.multiple_of(part * w_cols, w_cols), w_cols)
        return pltpu.make_async_copy(kbuf.at[:, cols], out_hbm.at[0, :, cols], out_sem.at[part])

    def project(low, high, first=False, last=False):
        depth = pl.ds(low * width, (high - low) * width)

        def part_of(part, _):
            cols = pl.ds(pl.multiple_of(part * w_cols, w_cols), w_cols)
            total = jnp.dot(
                att[:, depth], weight[part, depth, :], preferred_element_type=jnp.float32
            )
            if not first:
                total = total + acc[:, cols]
            if last:
                kbuf[:, cols] = total.astype(jnp.bfloat16)
                store(part).start()
            else:
                acc[:, cols] = total
            return 0

        lax.fori_loop(0, columns, part_of, 0)

    half = groups // 2
    for turn in range(groups + 2):
        if 0 <= turn - 1 < groups:
            frame_state(turn - 1)
        if 0 <= turn - 2 < groups:
            attend(turn - 2)
        if turn == 2:
            spread_groups()
        if turn == half + 1:
            forward_weight()
        if turn == half + 2:
            await_weight()
            project(0, half, first=True)
        if turn == half + 3:
            project(half, half + 2)
        if turn > half + 3:
            project(turn - 2, turn - 1, last=turn == groups + 1)
        if turn < groups:
            arrive(turn)

    for part in range(columns):
        store(part).wait()
        w_near_copy(part, tok).wait_send()
    for step in range(1, chips):
        w_far_copy(step, tok).wait_send()
        for hop in range(columns):
            if 0 < hop < n_tm:
                w_spread_copy(step, hop, column).wait_send()
            elif hop:
                spread_send(step, hop).wait_send()
            w_forward_copy(step, hop, far_source(step)).wait_send()
    for g in range(groups):
        near_copy(g, tok).wait_send()
        for step in range(1, chips):
            far_copy(g, step, tok).wait_send()
            forward_copy(g, step, far_source(step)).wait_send()
        for step in range(1, n_tm):
            state_copy(g, step).wait_send()
    for step in range(1, n_tok):
        gain_copy(step, tok).wait_send()


def on_device(n_tok, n_tm, columns, queries, keys, values, block_index, norm_gain, out_weight):
    rows, model_width = queries.shape[1:]
    kblk = block_index.shape[2]
    heads = model_width // HEAD_DIM
    groups = heads // GROUP_HEADS
    chips = n_tok // 2
    blocks = n_tok * rows // BLK
    gain_rows = jnp.broadcast_to(norm_gain.astype(jnp.float32)[None], (8, norm_gain.shape[0]))
    dma = pltpu.SemaphoreType.DMA
    return pl.pallas_call(
        functools.partial(mix_kernel, n_tok, n_tm, columns, groups, kblk),
        out_shape=jax.ShapeDtypeStruct((1, rows, model_width), jnp.bfloat16),
        in_specs=[
            pl.BlockSpec(memory_space=pltpu.SMEM),
            pl.BlockSpec(memory_space=pltpu.VMEM),
            pl.BlockSpec(memory_space=pl.ANY),
            pl.BlockSpec(memory_space=pl.ANY),
            pl.BlockSpec(memory_space=pl.ANY),
            pl.BlockSpec(memory_space=pl.ANY),
        ],
        out_specs=pl.BlockSpec(memory_space=pl.ANY),
        scratch_shapes=[
            pltpu.VMEM((blocks, GROUP_HEADS, HEAD_DIM, HEAD_DIM), jnp.bfloat16)
            for _ in range(groups)
        ] + [
            pltpu.VMEM((rows, model_width), jnp.bfloat16),
            pltpu.VMEM((rows, model_width), jnp.bfloat16),
            pltpu.VMEM((rows, model_width), jnp.bfloat16),
            pltpu.VMEM((rows, model_width), jnp.bfloat16),
            pltpu.VMEM((columns, model_width, model_width // columns), jnp.bfloat16),
            pltpu.VMEM((rows, model_width), jnp.float32),
            pltpu.VMEM((n_tok,) + gain_rows.shape, jnp.float32),
            pltpu.VMEM((groups, GROUP_HEADS, HEAD_DIM, HEAD_DIM), jnp.bfloat16),
            pltpu.VMEM((groups, n_tm, GROUP_HEADS, HEAD_DIM, HEAD_DIM), jnp.bfloat16),
            pltpu.VMEM((GROUP_HEADS, HEAD_DIM, HEAD_DIM), jnp.float32),
            dma((3, groups)),
            dma(()),
            dma((n_tok,)),
            dma((n_tok,)),
            dma((groups, chips)),
            dma((groups, chips)),
            dma((groups,)),
            dma((groups,)),
            dma((groups, chips)),
            dma((groups, chips)),
            dma((groups, n_tm)),
            dma((groups, n_tm)),
            dma((columns,)),
            dma((columns,)),
            dma((columns,)),
            dma((columns,)),
            dma((chips,)),
            dma((chips,)),
            dma((chips, columns)),
            dma((chips, columns)),
            dma((chips, columns)),
            dma((chips, columns)),
        ],
        compiler_params=pltpu.CompilerParams(
            collective_id=0, has_side_effects=True, vmem_limit_bytes=60 * 1024 * 1024
        ),
        cost_estimate=pl.CostEstimate(
            flops=8 * rows * model_width * HEAD_DIM, bytes_accessed=400_000_000, transcendentals=0
        ),
    )(block_index, gain_rows, queries, keys, values, out_weight)


def solution(mesh):
    in_specs = (
        P(("groups", "tm"), "tok", None),
        P(("groups", "tm"), "tok", None),
        P(("groups", "tm"), "tok", None),
        P(("groups", "tm"), None, None),
        P("tok"),
        P("tok", None),
    )
    out_specs = P(("groups", "tm"), "tok", None)
    return jax.shard_map(
        functools.partial(on_device, mesh.shape["tok"], mesh.shape["tm"], mesh.shape["groups"] * mesh.shape["tm"]),
        mesh=mesh, in_specs=in_specs, out_specs=out_specs, check_vma=False,
    )
```
